32 devices in a mesh: groups: 2 (over y), ctx: 8 (over z, x), mp: 2 (over core).
Axes of the slice: x: 2, y: 2, z: 4, core: 2. Of those that a mesh axis runs over, the one named last changes fastest.
Arguments:
- queries: bfloat16 [4096, 2048], P(('groups', 'ctx'), 'mp'), parts along dimension 0, may hold values from -9 to 9
- keys_values: bfloat16 [2, 4096, 1024], P(None, ('groups', 'ctx'), 'mp'), parts along dimension 1, may hold values from -9 to 9
- out_grad: bfloat16 [4096, 2048], P(('groups', 'ctx'), 'mp'), parts along dimension 0, may hold values from -6 to 6
- doc_ids: int32 [4096], P(('groups', 'ctx')), parts along dimension 0, may hold values from 0 to 4, as said below
Outputs:
- attended: bfloat16 [4096, 2048], P(('groups', 'ctx'), 'mp'), parts along dimension 0
- query_grad: bfloat16 [4096, 2048], P(('groups', 'ctx'), 'mp'), parts along dimension 0
- pair_grad: bfloat16 [2, 4096, 1024], P(None, ('groups', 'ctx'), 'mp'), parts along dimension 1
The draws below stay inside these ranges and needn't reach their ends.
There are 2 independent parts, one for each index of `groups`. The reference program is written for one: setup_inputs(seed, part) draws one part's arguments, and reference() takes and returns one part's arrays. A program takes and returns all parts, laid end to end along the dimension named above; each array names one. Nothing has to cross between parts.
Inputs may be any that keep to these rules, and one draw needn't show every extreme that they name: `doc_ids`: the sequence is a run of whole documents; all tokens of one document share a label, and the label rises by one from each document to the next, modulo 5, starting at 0. Every document holds at least 128 tokens (the first and the last may be shorter) and at most 512, and at least one holds exactly that many.
All inputs are finite; a program needn't handle non-finite values.
Results may differ from the reference program's by a relative error of at most 0.01.
Values may be sent and summed in bfloat16 or wider, within the bound.
A program may use at most 64 MiB of HBM per device.

```python
import jax
import jax.numpy as jnp
from jax import lax

HQ = 16
HK = 8
HD = 128
TOK_DEV = 256
DEPTH = 2
LENGTH = 2048
DOCS = 20
N_CTX = 8


def draw_doc_ids(key, part):
    key = jax.random.fold_in(key, 7)
    key_lengths, key_offset = jax.random.split(key)
    longest = DEPTH * TOK_DEV
    lengths = jax.random.randint(key_lengths, (DOCS - 1,), longest // 4, longest + 1)
    forced = jnp.arange(DOCS - 1) % 3 == 0
    lengths = jnp.where(forced, longest, lengths).astype(jnp.int32)
    offset = jax.random.randint(key_offset, (1,), 1, TOK_DEV).astype(jnp.int32)
    bounds = offset + jnp.cumsum(lengths) - lengths
    positions = jnp.arange(TOK_DEV * N_CTX, dtype=jnp.int32)
    counted = jnp.sum((bounds[None, :] <= positions[:, None]).astype(jnp.int32), axis=1).astype(jnp.int32)
    return (counted % (DEPTH + 3)).astype(jnp.int32)


def steps_of(key, extent, shards, smallest, high):
    gain = 1.0
    for dim, shards_of in shards:
        steps = jax.random.uniform(jax.random.fold_in(jax.random.fold_in(key, 6), dim), (shards_of,), jnp.float32, smallest / len(shards), high / len(shards))
        gain = gain * jnp.repeat(jnp.exp(steps), extent[dim] // shards_of).reshape((-1,) + (1,) * (len(extent) - 1 - dim))
    return gain


def gaussian(key, shape, deviation, most, shards=(), kind=jnp.bfloat16):
    values = jax.random.normal(key, shape, jnp.float32) * deviation
    if len(shards) > 0:
        values = steps_of(key, shape, shards, -0.22, 0.18) * values
    return jnp.clip(values, min=-most, max=most).astype(kind)


def setup_inputs(seed: int = 0, part: int = 0) -> dict:
    keys = jax.random.split(jax.random.key(seed), 5)
    own_keys = jax.random.split(jax.random.fold_in(keys[4], part), 5)
    queries = gaussian(own_keys[0], (LENGTH, HQ * HD), 1.5, 9.0, ((0, 8), (1, 2)))
    keys_values = gaussian(own_keys[1], (2, LENGTH, HK * HD), 1.5, 9.0, ((1, 8), (2, 2)))
    out_grad = gaussian(own_keys[2], (LENGTH, HQ * HD), 1.0, 6.0, ((0, 8), (1, 2)))
    doc_ids = draw_doc_ids(jax.random.fold_in(jax.random.fold_in(keys[4], part), 71), part)
    return dict(queries=queries, keys_values=keys_values, out_grad=out_grad, doc_ids=doc_ids)


SCORE_SCALE = 144.0 ** -0.5
SOFT_CAP = 50.0


def capped_logits(query_heads, key_heads):
    logits = jnp.einsum('qhd,khd->hqk', query_heads.astype(jnp.float32), key_heads.astype(jnp.float32)) * SCORE_SCALE
    return SOFT_CAP * jnp.tanh(logits / SOFT_CAP)


def reference(queries, keys_values, out_grad, doc_ids):
    length = queries.shape[0]
    group_size = HQ // HK
    reach_rows = DEPTH * TOK_DEV
    span_width = reach_rows + TOK_DEV
    query_all = queries.reshape(length, HQ, HD)
    grad_all = out_grad.reshape(length, HQ, HD)
    padded_pairs = jnp.concatenate([jnp.zeros((2, reach_rows, HK * HD), jnp.bfloat16), keys_values], axis=1)
    padded_docs = jnp.concatenate([jnp.full((reach_rows,), -1, jnp.int32), doc_ids])

    def block_step(grad_sums, block_index):
        row_start = (block_index * TOK_DEV).astype(jnp.int32)
        query_block = lax.dynamic_slice_in_dim(query_all, row_start, TOK_DEV, 0)
        grad_block = lax.dynamic_slice_in_dim(grad_all, row_start, TOK_DEV, 0)
        query_doc = lax.dynamic_slice_in_dim(doc_ids, row_start, TOK_DEV, 0)
        window = lax.dynamic_slice_in_dim(padded_pairs, row_start, span_width, 1)
        key_doc = lax.dynamic_slice_in_dim(padded_docs, row_start, span_width, 0)
        query_pos = row_start + jnp.arange(TOK_DEV, dtype=jnp.int32)
        key_pos = row_start - reach_rows + jnp.arange(span_width, dtype=jnp.int32)
        allowed = (key_pos[None, :] <= query_pos[:, None]) & (key_pos[None, :] >= 0) & (key_doc[None, :] == query_doc[:, None])
        key_heads = jnp.repeat(window[0].reshape(span_width, HK, HD), group_size, axis=1)
        value_heads = jnp.repeat(window[1].reshape(span_width, HK, HD), group_size, axis=1)
        capped = capped_logits(query_block, key_heads)
        exp_scores = jnp.where(allowed[None], jnp.exp(capped), 0.0)
        denominator = jnp.sum(exp_scores, axis=2)
        exp_rounded = lax.optimization_barrier(exp_scores.astype(jnp.bfloat16)).astype(jnp.float32)
        numerator = jnp.einsum('hqk,khd->qhd', exp_rounded, value_heads.astype(jnp.float32))
        attended = (numerator / denominator.T[:, :, None]).astype(jnp.bfloat16)
        attended_wide = lax.optimization_barrier(attended).astype(jnp.float32)
        grad_dot = jnp.sum(grad_block.astype(jnp.float32) * attended_wide, axis=2)
        probability = exp_scores / denominator[:, :, None]
        grad_prob = jnp.einsum('qhd,khd->hqk', grad_block.astype(jnp.float32), value_heads.astype(jnp.float32))
        grad_logit = probability * (grad_prob - grad_dot.T[:, :, None]) * (1.0 - (capped / SOFT_CAP) ** 2)
        grad_logit = lax.optimization_barrier(grad_logit.astype(jnp.bfloat16)).astype(jnp.float32)
        prob_rounded = lax.optimization_barrier(probability.astype(jnp.bfloat16)).astype(jnp.float32)
        query_grad = jnp.einsum('hqk,khd->qhd', grad_logit, key_heads.astype(jnp.float32)) * SCORE_SCALE
        key_grad = jnp.einsum('hqk,qhd->khd', grad_logit, query_block.astype(jnp.float32)) * SCORE_SCALE
        value_grad = jnp.einsum('hqk,qhd->khd', prob_rounded, grad_block.astype(jnp.float32))
        key_grad = key_grad.reshape(span_width, HK, group_size, HD).sum(axis=2).reshape(span_width, HK * HD)
        value_grad = value_grad.reshape(span_width, HK, group_size, HD).sum(axis=2).reshape(span_width, HK * HD)
        current = lax.dynamic_slice(grad_sums, (jnp.int32(0), row_start, jnp.int32(0)), (2, span_width, HK * HD))
        grad_sums = lax.dynamic_update_slice(grad_sums, current + jnp.stack([key_grad, value_grad]), (jnp.int32(0), row_start, jnp.int32(0)))
        return grad_sums, (attended.reshape(TOK_DEV, HQ * HD), query_grad.astype(jnp.bfloat16).reshape(TOK_DEV, HQ * HD))

    start_sums = jnp.zeros((2, reach_rows + length, HK * HD), jnp.float32)
    grad_sums, outputs = lax.scan(block_step, start_sums, jnp.arange(length // TOK_DEV, dtype=jnp.int32))
    attended_all = outputs[0].reshape(length, HQ * HD)
    query_grad_all = outputs[1].reshape(length, HQ * HD)
    return attended_all, query_grad_all, grad_sums[:, reach_rows:].astype(jnp.bfloat16)
```

```python
import functools
import math

import jax
import jax.numpy as jnp
from jax import lax
from jax.experimental import pallas as pl
from jax.experimental.pallas import tpu as pltpu
from jax.sharding import PartitionSpec as P

HD = 128
DEPTH = 2
SCORE_SCALE = 144.0 ** (-0.5)
SOFT_CAP = 50.0
TANH_SCALE = SCORE_SCALE / SOFT_CAP
EXP2_SCALE = SOFT_CAP * math.log2(math.e)

MESH = pl.DeviceIdType.MESH
F32 = jnp.float32
BF16 = jnp.bfloat16


def dot_nt(a, b):
    return lax.dot_general(a, b, (((1,), (1,)), ((), ())), preferred_element_type=F32)


def dot_nn(a, b):
    return lax.dot_general(a, b, (((1,), (0,)), ((), ())), preferred_element_type=F32)


def kernel(
    n, rows, heads, group,
    q_ref, kv_ref, do_ref, doc_ref,
    att_ref, dq_ref, dkv_ref,
    kv_in, doc_in, grad_out, grad_in, mask, exps, weights, own,
    kv_send, kv_recv, doc_send, doc_recv, grad_send, grad_recv,
):
    me = lax.axis_index("ctx")
    barrier = pltpu.get_barrier_semaphore()
    for d in range(1, DEPTH + 1):
        @pl.when(me >= d)
        def _(d=d):
            pl.semaphore_signal(barrier, inc=1, device_id={"ctx": me - d}, device_id_type=MESH)

        @pl.when(me + d < n)
        def _(d=d):
            pl.semaphore_signal(barrier, inc=1, device_id={"ctx": me + d}, device_id_type=MESH)

    peers = jnp.minimum(me, DEPTH) + jnp.minimum(n - 1 - me, DEPTH)
    pl.semaphore_wait(barrier, peers)

    def doc_copy(d):
        return pltpu.make_async_remote_copy(
            src_ref=doc_ref, dst_ref=doc_in.at[d - 1],
            send_sem=doc_send.at[d - 1], recv_sem=doc_recv.at[d - 1],
            device_id={"ctx": me + d}, device_id_type=MESH,
        )

    def head_cols(h):
        return pl.ds(pl.multiple_of(h * HD, HD), HD)

    def kv_copy(d, h):
        return pltpu.make_async_remote_copy(
            src_ref=kv_ref.at[:, :, head_cols(h)], dst_ref=kv_in.at[d - 1, h],
            send_sem=kv_send.at[d - 1, h], recv_sem=kv_recv.at[d - 1, h],
            device_id={"ctx": me + d}, device_id_type=MESH,
        )

    def grad_copy(d, h):
        return pltpu.make_async_remote_copy(
            src_ref=grad_out.at[d - 1, h], dst_ref=grad_in.at[d - 1, h],
            send_sem=grad_send.at[d - 1, h], recv_sem=grad_recv.at[d - 1, h],
            device_id={"ctx": me - d}, device_id_type=MESH,
        )

    for d in range(1, DEPTH + 1):
        @pl.when(me + d < n)
        def _(d=d):
            doc_copy(d).start()

    for h in range(heads):
        for d in range(1, DEPTH + 1):
            @pl.when(me + d < n)
            def _(d=d, h=h):
                kv_copy(d, h).start()

    for d in range(1, DEPTH + 1):
        @pl.when(me < d)
        def _(d=d):
            kv_in[d - 1] = jnp.zeros(kv_in.shape[1:], BF16)
            doc_in[d - 1] = jnp.full(doc_in.shape[1:], -1, jnp.int32)

        @pl.when(me + d >= n)
        def _(d=d):
            grad_in[d - 1] = jnp.zeros(grad_in.shape[1:], BF16)

    query_doc = jnp.broadcast_to(doc_ref[...].astype(F32), (rows, rows))

    def key_column(docs):
        column = jnp.transpose(jnp.broadcast_to(docs.astype(F32), (HD, rows)))
        return jnp.concatenate([column] * (rows // HD), axis=1)

    key_index = lax.broadcasted_iota(jnp.int32, (rows, rows), 0)
    query_index = lax.broadcasted_iota(jnp.int32, (rows, rows), 1)
    mask[0] = jnp.where(
        (key_column(doc_ref[...]) == query_doc) & (key_index <= query_index), 1.0, 0.0
    )
    for d in range(1, DEPTH + 1):
        @pl.when(me >= d)
        def _(d=d):
            doc_copy(d).wait_recv()

        mask[d] = jnp.where(key_column(doc_in[d - 1]) == query_doc, 1.0, 0.0)

    def head_step(h, carry):
        cols = head_cols(h)
        query_cols = [head_cols(h * group + g) for g in range(group)]
        queries = jnp.concatenate([q_ref[:, c] for c in query_cols], axis=0)
        grads = jnp.concatenate([do_ref[:, c] for c in query_cols], axis=0)
        width = group * rows
        numerator = jnp.zeros((HD, width), F32)
        sums = [jnp.zeros((1, rows), F32) for _ in range(group)]

        def block(d, which):
            if d == 0:
                return kv_ref[which, :, cols]
            return kv_in[d - 1, h, which]

        for d in range(DEPTH + 1):
            if d > 0:
                @pl.when(me >= d)
                def _(d=d):
                    kv_copy(d, h).wait_recv()

            scores = dot_nt(block(d, 0), queries)
            for g in range(group):
                span = slice(g * rows, (g + 1) * rows)
                capped = jnp.tanh(scores[:, span] * TANH_SCALE)
                exp_scores = jnp.exp2(capped * EXP2_SCALE) * mask[d]
                weights[d, :, span] = exp_scores - exp_scores * (capped * capped)
                sums[g] = sums[g] + jnp.sum(exp_scores, axis=0, keepdims=True)
                exps[d, :, span] = exp_scores.astype(BF16)
            numerator = numerator + dot_nn(jnp.transpose(block(d, 1)), exps[d])

        inverse = 1.0 / jnp.concatenate(sums, axis=1)
        attended = (numerator * inverse).astype(BF16)
        grad_dot = jnp.sum(
            jnp.transpose(grads).astype(F32) * attended.astype(F32), axis=0, keepdims=True
        )
        for g in range(group):
            att_ref[:, query_cols[g]] = jnp.transpose(attended[:, g * rows:(g + 1) * rows])
        inverse_column = jnp.transpose(jnp.broadcast_to(inverse, (HD, width)))
        grads_scaled = (grads.astype(F32) * inverse_column).astype(BF16)

        query_sum = jnp.zeros((HD, width), F32)
        for d in range(DEPTH, -1, -1):
            grad_prob = dot_nt(block(d, 1), grads)
            grad_logit = (weights[d] * ((grad_prob - grad_dot) * inverse)).astype(BF16)
            key_grad = dot_nn(grad_logit, queries) * SCORE_SCALE
            value_grad = dot_nn(exps[d], grads_scaled)
            if d == 0:
                own[h, 0] = key_grad
                own[h, 1] = value_grad
            else:
                grad_out[d - 1, h, 0] = key_grad.astype(BF16)
                grad_out[d - 1, h, 1] = value_grad.astype(BF16)

                @pl.when(me >= d)
                def _(d=d):
                    grad_copy(d, h).start()

            query_sum = query_sum + dot_nn(jnp.transpose(block(d, 0)), grad_logit)
        query_grad = (query_sum * SCORE_SCALE).astype(BF16)
        for g in range(group):
            dq_ref[:, query_cols[g]] = jnp.transpose(query_grad[:, g * rows:(g + 1) * rows])
        return carry

    lax.fori_loop(0, heads, head_step, 0)

    def finish(h, carry):
        for d in range(1, DEPTH + 1):
            @pl.when(me + d < n)
            def _(d=d):
                grad_copy(d, h).wait_recv()

        total = own[h]
        for d in range(1, DEPTH + 1):
            total = total + grad_in[d - 1, h].astype(F32)
        dkv_ref[:, :, head_cols(h)] = total.astype(BF16)
        return carry

    lax.fori_loop(0, heads, finish, 0)

    for d in range(1, DEPTH + 1):
        @pl.when(me + d < n)
        def _(d=d):
            doc_copy(d).wait_send()

    def drain(h, carry):
        for d in range(1, DEPTH + 1):
            @pl.when(me + d < n)
            def _(d=d):
                kv_copy(d, h).wait_send()

            @pl.when(me >= d)
            def _(d=d):
                grad_copy(d, h).wait_send()
        return carry

    lax.fori_loop(0, heads, drain, 0)


def per_device(queries, keys_values, out_grad, doc_ids):
    rows = queries.shape[0]
    heads = keys_values.shape[2] // HD
    group = queries.shape[1] // HD // heads
    n = lax.axis_size("ctx")
    slot = (DEPTH, heads, 2, rows, HD)
    vmem = pl.BlockSpec(memory_space=pltpu.VMEM)
    dma = pltpu.SemaphoreType.DMA
    return pl.pallas_call(
        functools.partial(kernel, n, rows, heads, group),
        out_shape=(
            jax.ShapeDtypeStruct(queries.shape, BF16),
            jax.ShapeDtypeStruct(queries.shape, BF16),
            jax.ShapeDtypeStruct(keys_values.shape, BF16),
        ),
        in_specs=[vmem] * 4,
        out_specs=(vmem,) * 3,
        scratch_shapes=[
            pltpu.VMEM(slot, BF16),
            pltpu.VMEM((DEPTH, 1, rows), jnp.int32),
            pltpu.VMEM(slot, BF16),
            pltpu.VMEM(slot, BF16),
            pltpu.VMEM((DEPTH + 1, rows, rows), F32),
            pltpu.VMEM((DEPTH + 1, rows, group * rows), BF16),
            pltpu.VMEM((DEPTH + 1, rows, group * rows), F32),
            pltpu.VMEM((heads, 2, rows, HD), F32),
            dma((DEPTH, heads)), dma((DEPTH, heads)),
            dma((DEPTH,)), dma((DEPTH,)),
            dma((DEPTH, heads)), dma((DEPTH, heads)),
        ],
        compiler_params=pltpu.CompilerParams(
            collective_id=0, has_side_effects=True, vmem_limit_bytes=40 * 1024 * 1024
        ),
        name="packed_attention",
    )(queries, keys_values, out_grad, doc_ids.reshape(1, rows))


def solution(mesh):
    return jax.shard_map(
        per_device,
        mesh=mesh,
        in_specs=(
            P(("groups", "ctx"), "mp"),
            P(None, ("groups", "ctx"), "mp"),
            P(("groups", "ctx"), "mp"),
            P(("groups", "ctx")),
        ),
        out_specs=(
            P(("groups", "ctx"), "mp"),
            P(("groups", "ctx"), "mp"),
            P(None, ("groups", "ctx"), "mp"),
        ),
        check_vma=False,
    )
```

```python
import functools
import math

import jax
import jax.numpy as jnp
from jax import lax
from jax.experimental import pallas as pl
from jax.experimental.pallas import tpu as pltpu
from jax.sharding import PartitionSpec as P

HD = 128
DEPTH = 2
SCORE_SCALE = 144.0 ** (-0.5)
SOFT_CAP = 50.0
TANH_SCALE = SCORE_SCALE / SOFT_CAP
EXP2_SCALE = SOFT_CAP * math.log2(math.e)

MESH = pl.DeviceIdType.MESH
F32 = jnp.float32
BF16 = jnp.bfloat16


def dot_nt(a, b):
    return lax.dot_general(a, b, (((1,), (1,)), ((), ())), preferred_element_type=F32)


def dot_nn(a, b):
    return lax.dot_general(a, b, (((1,), (0,)), ((), ())), preferred_element_type=F32)


def kernel(
    n, rows, heads, group,
    q_hbm, kv_hbm, do_hbm, doc_hbm,
    att_ref, dq_ref, dkv_ref,
    q_ref, kv_ref, do_ref, doc_ref,
    kv_in, doc_in, grad_out, grad_in, mask, exps, weights, own,
    load_sem, kv_send, kv_recv, doc_send, doc_recv, grad_send, grad_recv,
):
    me = lax.axis_index("ctx")
    loads = [
        pltpu.make_async_copy(src, dst, load_sem.at[k])
        for k, (src, dst) in enumerate(
            ((kv_hbm, kv_ref), (doc_hbm, doc_ref), (q_hbm, q_ref), (do_hbm, do_ref))
        )
    ]
    for load in loads:
        load.start()

    barrier = pltpu.get_barrier_semaphore()
    for d in range(1, DEPTH + 1):
        @pl.when(me >= d)
        def _(d=d):
            pl.semaphore_signal(barrier, inc=1, device_id={"ctx": me - d}, device_id_type=MESH)

        @pl.when(me + d < n)
        def _(d=d):
            pl.semaphore_signal(barrier, inc=1, device_id={"ctx": me + d}, device_id_type=MESH)

    peers = jnp.minimum(me, DEPTH) + jnp.minimum(n - 1 - me, DEPTH)
    pl.semaphore_wait(barrier, peers)

    def doc_copy(d):
        return pltpu.make_async_remote_copy(
            src_ref=doc_hbm, dst_ref=doc_in.at[d - 1],
            send_sem=doc_send.at[d - 1], recv_sem=doc_recv.at[d - 1],
            device_id={"ctx": me + d}, device_id_type=MESH,
        )

    def head_cols(h):
        return pl.ds(pl.multiple_of(h * HD, HD), HD)

    def kv_copy(d, h):
        return pltpu.make_async_remote_copy(
            src_ref=kv_hbm.at[:, :, head_cols(h)], dst_ref=kv_in.at[d - 1, h],
            send_sem=kv_send.at[d - 1, h], recv_sem=kv_recv.at[d - 1, h],
            device_id={"ctx": me + d}, device_id_type=MESH,
        )

    def grad_copy(d, h):
        return pltpu.make_async_remote_copy(
            src_ref=grad_out.at[d - 1, h], dst_ref=grad_in.at[d - 1, h],
            send_sem=grad_send.at[d - 1, h], recv_sem=grad_recv.at[d - 1, h],
            device_id={"ctx": me - d}, device_id_type=MESH,
        )

    for d in range(1, DEPTH + 1):
        @pl.when(me + d < n)
        def _(d=d):
            doc_copy(d).start()

    for h in range(heads):
        for d in range(1, DEPTH + 1):
            @pl.when(me + d < n)
            def _(d=d, h=h):
                kv_copy(d, h).start()

    for d in range(1, DEPTH + 1):
        @pl.when(me < d)
        def _(d=d):
            kv_in[d - 1] = jnp.zeros(kv_in.shape[1:], BF16)
            doc_in[d - 1] = jnp.full(doc_in.shape[1:], -1, jnp.int32)

        @pl.when(me + d >= n)
        def _(d=d):
            grad_in[d - 1] = jnp.zeros(grad_in.shape[1:], BF16)

    for load in loads:
        load.wait()

    query_doc = jnp.broadcast_to(doc_ref[...].astype(F32), (rows, rows))

    def key_column(docs):
        column = jnp.transpose(jnp.broadcast_to(docs.astype(F32), (HD, rows)))
        return jnp.concatenate([column] * (rows // HD), axis=1)

    key_index = lax.broadcasted_iota(jnp.int32, (rows, rows), 0)
    query_index = lax.broadcasted_iota(jnp.int32, (rows, rows), 1)
    mask[0] = jnp.where(
        (key_column(doc_ref[...]) == query_doc) & (key_index <= query_index), 1.0, 0.0
    )
    for d in range(1, DEPTH + 1):
        @pl.when(me >= d)
        def _(d=d):
            doc_copy(d).wait_recv()

        mask[d] = jnp.where(key_column(doc_in[d - 1]) == query_doc, 1.0, 0.0)

    def head_step(h, carry):
        cols = head_cols(h)
        query_cols = [head_cols(h * group + g) for g in range(group)]
        queries = jnp.concatenate([q_ref[:, c] for c in query_cols], axis=0)
        grads = jnp.concatenate([do_ref[:, c] for c in query_cols], axis=0)
        width = group * rows
        numerator = jnp.zeros((HD, width), F32)
        sums = [jnp.zeros((1, rows), F32) for _ in range(group)]

        def block(d, which):
            if d == 0:
                return kv_ref[which, :, cols]
            return kv_in[d - 1, h, which]

        for d in range(DEPTH + 1):
            if d > 0:
                @pl.when(me >= d)
                def _(d=d):
                    kv_copy(d, h).wait_recv()

            scores = dot_nt(block(d, 0), queries)
            for g in range(group):
                span = slice(g * rows, (g + 1) * rows)
                capped = jnp.tanh(scores[:, span] * TANH_SCALE)
                exp_scores = jnp.exp2(capped * EXP2_SCALE) * mask[d]
                weights[d, :, span] = exp_scores - exp_scores * (capped * capped)
                sums[g] = sums[g] + jnp.sum(exp_scores, axis=0, keepdims=True)
                exps[d, :, span] = exp_scores.astype(BF16)
            numerator = numerator + dot_nn(jnp.transpose(block(d, 1)), exps[d])

        inverse = 1.0 / jnp.concatenate(sums, axis=1)
        attended = (numerator * inverse).astype(BF16)
        grad_dot = jnp.sum(
            jnp.transpose(grads).astype(F32) * attended.astype(F32), axis=0, keepdims=True
        )
        for g in range(group):
            att_ref[:, query_cols[g]] = jnp.transpose(attended[:, g * rows:(g + 1) * rows])
        inverse_column = jnp.transpose(jnp.broadcast_to(inverse, (HD, width)))
        grads_scaled = (grads.astype(F32) * inverse_column).astype(BF16)

        query_sum = jnp.zeros((HD, width), F32)
        for d in range(DEPTH, -1, -1):
            grad_prob = dot_nt(block(d, 1), grads)
            grad_logit = (weights[d] * ((grad_prob - grad_dot) * inverse)).astype(BF16)
            key_grad = dot_nn(grad_logit, queries) * SCORE_SCALE
            value_grad = dot_nn(exps[d], grads_scaled)
            if d == 0:
                own[h, 0] = key_grad
                own[h, 1] = value_grad
            else:
                grad_out[d - 1, h, 0] = key_grad.astype(BF16)
                grad_out[d - 1, h, 1] = value_grad.astype(BF16)

                @pl.when(me >= d)
                def _(d=d):
                    grad_copy(d, h).start()

            query_sum = query_sum + dot_nn(jnp.transpose(block(d, 0)), grad_logit)
        query_grad = (query_sum * SCORE_SCALE).astype(BF16)
        for g in range(group):
            dq_ref[:, query_cols[g]] = jnp.transpose(query_grad[:, g * rows:(g + 1) * rows])
        return carry

    lax.fori_loop(0, heads, head_step, 0)

    def finish(h, carry):
        for d in range(1, DEPTH + 1):
            @pl.when(me + d < n)
            def _(d=d):
                grad_copy(d, h).wait_recv()

        total = own[h]
        for d in range(1, DEPTH + 1):
            total = total + grad_in[d - 1, h].astype(F32)
        dkv_ref[:, :, head_cols(h)] = total.astype(BF16)
        return carry

    lax.fori_loop(0, heads, finish, 0)

    for d in range(1, DEPTH + 1):
        @pl.when(me + d < n)
        def _(d=d):
            doc_copy(d).wait_send()

    def drain(h, carry):
        for d in range(1, DEPTH + 1):
            @pl.when(me + d < n)
            def _(d=d):
                kv_copy(d, h).wait_send()

            @pl.when(me >= d)
            def _(d=d):
                grad_copy(d, h).wait_send()
        return carry

    lax.fori_loop(0, heads, drain, 0)


def per_device(queries, keys_values, out_grad, doc_ids):
    rows = queries.shape[0]
    heads = keys_values.shape[2] // HD
    group = queries.shape[1] // HD // heads
    n = lax.axis_size("ctx")
    slot = (DEPTH, heads, 2, rows, HD)
    vmem = pl.BlockSpec(memory_space=pltpu.VMEM)
    dma = pltpu.SemaphoreType.DMA
    return pl.pallas_call(
        functools.partial(kernel, n, rows, heads, group),
        out_shape=(
            jax.ShapeDtypeStruct(queries.shape, BF16),
            jax.ShapeDtypeStruct(queries.shape, BF16),
            jax.ShapeDtypeStruct(keys_values.shape, BF16),
        ),
        in_specs=[pl.BlockSpec(memory_space=pltpu.HBM)] * 4,
        out_specs=(vmem,) * 3,
        scratch_shapes=[
            pltpu.VMEM(queries.shape, BF16),
            pltpu.VMEM(keys_values.shape, BF16),
            pltpu.VMEM(queries.shape, BF16),
            pltpu.VMEM((1, rows), jnp.int32),
            pltpu.VMEM(slot, BF16),
            pltpu.VMEM((DEPTH, 1, rows), jnp.int32),
            pltpu.VMEM(slot, BF16),
            pltpu.VMEM(slot, BF16),
            pltpu.VMEM((DEPTH + 1, rows, rows), F32),
            pltpu.VMEM((DEPTH + 1, rows, group * rows), BF16),
            pltpu.VMEM((DEPTH + 1, rows, group * rows), F32),
            pltpu.VMEM((heads, 2, rows, HD), F32),
            dma((4,)),
            dma((DEPTH, heads)), dma((DEPTH, heads)),
            dma((DEPTH,)), dma((DEPTH,)),
            dma((DEPTH, heads)), dma((DEPTH, heads)),
        ],
        compiler_params=pltpu.CompilerParams(
            collective_id=0, has_side_effects=True, vmem_limit_bytes=63 * 1024 * 1024
        ),
        name="packed_attention",
    )(queries, keys_values, out_grad, doc_ids.reshape(1, rows))


def solution(mesh):
    return jax.shard_map(
        per_device,
        mesh=mesh,
        in_specs=(
            P(("groups", "ctx"), "mp"),
            P(None, ("groups", "ctx"), "mp"),
            P(("groups", "ctx"), "mp"),
            P(("groups", "ctx")),
        ),
        out_specs=(
            P(("groups", "ctx"), "mp"),
            P(("groups", "ctx"), "mp"),
            P(None, ("groups", "ctx"), "mp"),
        ),
        check_vma=False,
    )
```

```python
import functools
import math

import jax
import jax.numpy as jnp
from jax import lax
from jax.experimental import pallas as pl
from jax.experimental.pallas import tpu as pltpu
from jax.sharding import PartitionSpec as P

HD = 128
DEPTH = 2
SCORE_SCALE = 144.0 ** (-0.5)
SOFT_CAP = 50.0
TANH_SCALE = SCORE_SCALE / SOFT_CAP
EXP2_SCALE = SOFT_CAP * math.log2(math.e)

MESH = pl.DeviceIdType.MESH
F32 = jnp.float32
BF16 = jnp.bfloat16


def dot_nt(a, b):
    return lax.dot_general(a, b, (((1,), (1,)), ((), ())), preferred_element_type=F32)


def dot_nn(a, b):
    return lax.dot_general(a, b, (((1,), (0,)), ((), ())), preferred_element_type=F32)


def kernel(
    n, rows, heads, group,
    q_hbm, kv_hbm, do_hbm, doc_hbm,
    att_ref, dq_ref, dkv_ref,
    q_ref, kv_ref, do_ref, doc_ref,
    kv_in, doc_in, grad_out, grad_in, mask, exps, weights, own,
    load_sem, kv_send, kv_recv, doc_send, doc_recv, grad_send, grad_recv,
):
    me = lax.axis_index("ctx")
    loads = [
        pltpu.make_async_copy(src, dst, load_sem.at[k])
        for k, (src, dst) in enumerate(
            ((kv_hbm, kv_ref), (doc_hbm, doc_ref), (q_hbm, q_ref), (do_hbm, do_ref))
        )
    ]
    for load in loads:
        load.start()

    barrier = pltpu.get_barrier_semaphore()
    for d in range(1, DEPTH + 1):
        @pl.when(me >= d)
        def _(d=d):
            pl.semaphore_signal(barrier, inc=1, device_id={"ctx": me - d}, device_id_type=MESH)

        @pl.when(me + d < n)
        def _(d=d):
            pl.semaphore_signal(barrier, inc=1, device_id={"ctx": me + d}, device_id_type=MESH)

    peers = jnp.minimum(me, DEPTH) + jnp.minimum(n - 1 - me, DEPTH)
    pl.semaphore_wait(barrier, peers)

    def doc_copy(d):
        return pltpu.make_async_remote_copy(
            src_ref=doc_hbm, dst_ref=doc_in.at[d - 1],
            send_sem=doc_send.at[d - 1], recv_sem=doc_recv.at[d - 1],
            device_id={"ctx": me + d}, device_id_type=MESH,
        )

    def head_cols(h):
        return pl.ds(pl.multiple_of(h * HD, HD), HD)

    def kv_copy(d, h):
        return pltpu.make_async_remote_copy(
            src_ref=kv_hbm.at[:, :, head_cols(h)], dst_ref=kv_in.at[d - 1, h],
            send_sem=kv_send.at[d - 1, h], recv_sem=kv_recv.at[d - 1, h],
            device_id={"ctx": me + d}, device_id_type=MESH,
        )

    def grad_copy(d, h, which):
        return pltpu.make_async_remote_copy(
            src_ref=grad_out.at[d - 1, h, which], dst_ref=grad_in.at[d - 1, h, which],
            send_sem=grad_send.at[d - 1, h, which], recv_sem=grad_recv.at[d - 1, h, which],
            device_id={"ctx": me - d}, device_id_type=MESH,
        )

    for d in range(1, DEPTH + 1):
        @pl.when(me + d < n)
        def _(d=d):
            doc_copy(d).start()

    for h in range(heads):
        for d in range(1, DEPTH + 1):
            @pl.when(me + d < n)
            def _(d=d, h=h):
                kv_copy(d, h).start()

    for d in range(1, DEPTH + 1):
        @pl.when(me < d)
        def _(d=d):
            kv_in[d - 1] = jnp.zeros(kv_in.shape[1:], BF16)
            doc_in[d - 1] = jnp.full(doc_in.shape[1:], -1, jnp.int32)

        @pl.when(me + d >= n)
        def _(d=d):
            grad_in[d - 1] = jnp.zeros(grad_in.shape[1:], BF16)

    for load in loads:
        load.wait()

    query_doc = jnp.broadcast_to(doc_ref[...].astype(F32), (rows, rows))

    def key_column(docs):
        column = jnp.transpose(jnp.broadcast_to(docs.astype(F32), (HD, rows)))
        return jnp.concatenate([column] * (rows // HD), axis=1)

    key_index = lax.broadcasted_iota(jnp.int32, (rows, rows), 0)
    query_index = lax.broadcasted_iota(jnp.int32, (rows, rows), 1)
    mask[0] = jnp.where(
        (key_column(doc_ref[...]) == query_doc) & (key_index <= query_index), 1.0, 0.0
    )
    for d in range(1, DEPTH + 1):
        @pl.when(me >= d)
        def _(d=d):
            doc_copy(d).wait_recv()

        mask[d] = jnp.where(key_column(doc_in[d - 1]) == query_doc, 1.0, 0.0)

    def head_step(h, carry):
        cols = head_cols(h)
        query_cols = [head_cols(h * group + g) for g in range(group)]
        queries = jnp.concatenate([q_ref[:, c] for c in query_cols], axis=0)
        grads = jnp.concatenate([do_ref[:, c] for c in query_cols], axis=0)
        width = group * rows
        numerator = jnp.zeros((HD, width), F32)
        sums = [jnp.zeros((1, rows), F32) for _ in range(group)]

        def block(d, which):
            if d == 0:
                return kv_ref[which, :, cols]
            return kv_in[d - 1, h, which]

        for d in range(DEPTH + 1):
            if d > 0:
                @pl.when(me >= d)
                def _(d=d):
                    kv_copy(d, h).wait_recv()

            scores = dot_nt(block(d, 0), queries)
            for g in range(group):
                span = slice(g * rows, (g + 1) * rows)
                capped = jnp.tanh(scores[:, span] * TANH_SCALE)
                exp_scores = jnp.exp2(capped * EXP2_SCALE) * mask[d]
                weights[d, :, span] = exp_scores - exp_scores * (capped * capped)
                sums[g] = sums[g] + jnp.sum(exp_scores, axis=0, keepdims=True)
                exps[d, :, span] = exp_scores.astype(BF16)
            numerator = numerator + dot_nn(jnp.transpose(block(d, 1)), exps[d])

        inverse = 1.0 / jnp.concatenate(sums, axis=1)
        attended = (numerator * inverse).astype(BF16)
        grad_dot = jnp.sum(
            jnp.transpose(grads).astype(F32) * attended.astype(F32), axis=0, keepdims=True
        )
        for g in range(group):
            att_ref[:, query_cols[g]] = jnp.transpose(attended[:, g * rows:(g + 1) * rows])
        inverse_column = jnp.transpose(jnp.broadcast_to(inverse, (HD, width)))
        grads_scaled = (grads.astype(F32) * inverse_column).astype(BF16)

        for d in range(DEPTH, 0, -1):
            grad_out[d - 1, h, 1] = dot_nn(exps[d], grads_scaled).astype(BF16)

            @pl.when(me >= d)
            def _(d=d):
                grad_copy(d, h, 1).start()

        own[h, 1] = dot_nn(exps[0], grads_scaled)
        query_sum = jnp.zeros((HD, width), F32)
        for d in range(DEPTH, -1, -1):
            grad_prob = dot_nt(block(d, 1), grads)
            grad_logit = (weights[d] * ((grad_prob - grad_dot) * inverse)).astype(BF16)
            key_grad = dot_nn(grad_logit, queries) * SCORE_SCALE
            if d == 0:
                own[h, 0] = key_grad
            else:
                grad_out[d - 1, h, 0] = key_grad.astype(BF16)

                @pl.when(me >= d)
                def _(d=d):
                    grad_copy(d, h, 0).start()

            query_sum = query_sum + dot_nn(jnp.transpose(block(d, 0)), grad_logit)
        query_grad = (query_sum * SCORE_SCALE).astype(BF16)
        for g in range(group):
            dq_ref[:, query_cols[g]] = jnp.transpose(query_grad[:, g * rows:(g + 1) * rows])
        return carry

    lax.fori_loop(0, heads, head_step, 0)

    def finish(h, carry):
        for d in range(1, DEPTH + 1):
            @pl.when(me + d < n)
            def _(d=d):
                for which in range(2):
                    grad_copy(d, h, which).wait_recv()

        total = own[h]
        for d in range(1, DEPTH + 1):
            total = total + grad_in[d - 1, h].astype(F32)
        dkv_ref[:, :, head_cols(h)] = total.astype(BF16)
        return carry

    lax.fori_loop(0, heads, finish, 0)

    for d in range(1, DEPTH + 1):
        @pl.when(me + d < n)
        def _(d=d):
            doc_copy(d).wait_send()

    def drain(h, carry):
        for d in range(1, DEPTH + 1):
            @pl.when(me + d < n)
            def _(d=d):
                kv_copy(d, h).wait_send()

            @pl.when(me >= d)
            def _(d=d):
                for which in range(2):
                    grad_copy(d, h, which).wait_send()
        return carry

    lax.fori_loop(0, heads, drain, 0)


def per_device(queries, keys_values, out_grad, doc_ids):
    rows = queries.shape[0]
    heads = keys_values.shape[2] // HD
    group = queries.shape[1] // HD // heads
    n = lax.axis_size("ctx")
    slot = (DEPTH, heads, 2, rows, HD)
    vmem = pl.BlockSpec(memory_space=pltpu.VMEM)
    dma = pltpu.SemaphoreType.DMA
    return pl.pallas_call(
        functools.partial(kernel, n, rows, heads, group),
        out_shape=(
            jax.ShapeDtypeStruct(queries.shape, BF16),
            jax.ShapeDtypeStruct(queries.shape, BF16),
            jax.ShapeDtypeStruct(keys_values.shape, BF16),
        ),
        in_specs=[pl.BlockSpec(memory_space=pltpu.HBM)] * 4,
        out_specs=(vmem,) * 3,
        scratch_shapes=[
            pltpu.VMEM(queries.shape, BF16),
            pltpu.VMEM(keys_values.shape, BF16),
            pltpu.VMEM(queries.shape, BF16),
            pltpu.VMEM((1, rows), jnp.int32),
            pltpu.VMEM(slot, BF16),
            pltpu.VMEM((DEPTH, 1, rows), jnp.int32),
            pltpu.VMEM(slot, BF16),
            pltpu.VMEM(slot, BF16),
            pltpu.VMEM((DEPTH + 1, rows, rows), F32),
            pltpu.VMEM((DEPTH + 1, rows, group * rows), BF16),
            pltpu.VMEM((DEPTH + 1, rows, group * rows), F32),
            pltpu.VMEM((heads, 2, rows, HD), F32),
            dma((4,)),
            dma((DEPTH, heads)), dma((DEPTH, heads)),
            dma((DEPTH,)), dma((DEPTH,)),
            dma((DEPTH, heads, 2)), dma((DEPTH, heads, 2)),
        ],
        compiler_params=pltpu.CompilerParams(
            collective_id=0, has_side_effects=True, vmem_limit_bytes=63 * 1024 * 1024
        ),
        name="packed_attention",
    )(queries, keys_values, out_grad, doc_ids.reshape(1, rows))


def solution(mesh):
    return jax.shard_map(
        per_device,
        mesh=mesh,
        in_specs=(
            P(("groups", "ctx"), "mp"),
            P(None, ("groups", "ctx"), "mp"),
            P(("groups", "ctx"), "mp"),
            P(("groups", "ctx")),
        ),
        out_specs=(
            P(("groups", "ctx"), "mp"),
            P(("groups", "ctx"), "mp"),
            P(None, ("groups", "ctx"), "mp"),
        ),
        check_vma=False,
    )
```
